256 devices in a mesh: dp: 16 (over y, z_lo), tensor: 16 (over z_hi, x, core).
Axes of the slice: x: 4, y: 4, z: 8 (z_hi: 2, z_lo: 4; z = z_hi * 4 + z_lo), core: 2. Of those that a mesh axis runs over, the one named last changes fastest.
Arguments:
- context: bfloat16 [8192, 6144], P('dp', 'tensor'), may hold values from -6 to 6
- w_out: bfloat16 [6144, 6144], P('tensor'), may hold values from -0.078125 to 0.078125
- encoder: bfloat16 [2048, 384], replicated, may hold values from -0.3125 to 0.3125
- decoder: bfloat16 [2048, 384], replicated, may hold values from -0.5 to 0.5
- cotangent: bfloat16 [8192, 6144], P(('dp', 'tensor')), may hold values from -6 to 6
Outputs:
- layer_out: bfloat16 [8192, 6144], P(('dp', 'tensor'))
- context_grad: bfloat16 [8192, 6144], P('dp', 'tensor')
- w_out_grad: float32 [6144, 6144], P('tensor', 'dp')
- encoder_grad: float32 [2048, 384], P(('dp', 'tensor'))
- decoder_grad: float32 [2048, 384], P(('dp', 'tensor'))
The draws below stay inside these ranges and needn't reach their ends.
All inputs are finite; a program needn't handle non-finite values.
Results may differ from the reference program's by a relative error of at most 0.02.
Values may be sent and summed in bfloat16 or wider, within the bound.
No kernel may reach another device: no remote copies, remote signals or barrier semaphores. Data moves between devices by JAX's collectives and lax.ppermute only.
A program may use at most 128 MiB of HBM per device.

```python
import jax
import jax.numpy as jnp
from jax import lax

D = 6144
C = 2048
GROUPS = 16
HD = 128
HEADS_DEV = 3
SEQ = 512
GROUP_D = 384
GROUP_C = 128
HID = 6144
TOKENS = 8192
N_DP = 16
N_TENSOR = 16


def levels(rng, extent, split, least, high):
    level = 1.0
    for dim, parts in split:
        steps = jax.random.uniform(jax.random.fold_in(jax.random.fold_in(rng, 6), dim), (parts,), jnp.float32, least / len(split), high / len(split))
        level = level * jnp.repeat(jnp.exp(steps), extent[dim] // parts).reshape((-1,) + (1,) * (len(extent) - 1 - dim))
    return level


def normal_values(own_key, dims, scale, limit, shards=(), kind=jnp.bfloat16):
    drawn = scale * jax.random.normal(own_key, dims, jnp.float32)
    if shards:
        drawn = drawn * levels(own_key, dims, shards, -0.22, 0.18)
    return jnp.clip(drawn, -limit, limit).astype(kind)


def setup_inputs(seed: int = 0) -> dict:
    arg_keys = jax.random.split(jax.random.key(seed), 6)
    context = normal_values(arg_keys[0], (TOKENS, HID), 1.0, 6.0, ((0, 16), (1, 16)))
    w_out = normal_values(arg_keys[1], (HID, D), HID ** -0.5, 0.078125, ((0, 16),))
    encoder = normal_values(arg_keys[2], (C, GROUP_D), GROUP_D ** -0.5, 0.3125)
    decoder = normal_values(arg_keys[3], (C, GROUP_D), GROUP_C ** -0.5, 0.5)
    cotangent = normal_values(arg_keys[4], (TOKENS, D), 1.0, 6.0, ((0, 256),))
    return dict(context=context, w_out=w_out, encoder=encoder, decoder=decoder, cotangent=cotangent)


def data_groups(first_factor, second_factor):
    def accumulate_group(running, position):
        offset = position * SEQ
        first_block = lax.dynamic_slice_in_dim(first_factor, offset, SEQ, 0)
        second_block = lax.dynamic_slice_in_dim(second_factor, offset, SEQ, 0)
        partial_value = lax.dot_general(first_block, second_block, (((0,), (0,)), ((), ())), preferred_element_type=jnp.float32)
        partial_value = lax.optimization_barrier(partial_value.astype(jnp.bfloat16))
        return running + partial_value.astype(jnp.float32), None

    starting = jnp.zeros((first_factor.shape[1], second_factor.shape[1]), jnp.float32)
    running, _ = lax.scan(accumulate_group, starting, jnp.arange(N_DP, dtype=jnp.int32))
    return running


def reference(context, w_out, encoder, decoder, cotangent):
    group_feat = D // GROUPS
    group_code = C // GROUPS
    enc_blocks = encoder.astype(jnp.float32).reshape(GROUPS, group_code, group_feat)
    dec_blocks = decoder.astype(jnp.float32).reshape(GROUPS, group_code, group_feat)
    cot_blocks = cotangent.astype(jnp.float32).reshape(TOKENS, GROUPS, group_feat)
    code_grad = jnp.einsum("tgd,gcd->tgc", cot_blocks, dec_blocks).astype(jnp.bfloat16)
    code_grad = lax.optimization_barrier(code_grad)
    grad_wide = code_grad.astype(jnp.float32)
    group_width = HEADS_DEV * HD

    def accumulate(carry, position):
        codes, enc_term = carry
        offset = position * group_width
        selected = lax.dynamic_slice_in_dim(context, offset, group_width, 1)
        weight_rows = lax.dynamic_slice_in_dim(w_out, offset, group_width, 0)
        partial_value = jnp.dot(selected, weight_rows, preferred_element_type=jnp.float32).astype(jnp.bfloat16)
        partial_value = lax.optimization_barrier(partial_value)
        partial_blocks = partial_value.astype(jnp.float32).reshape(TOKENS, GROUPS, group_feat)
        piece_code = jnp.einsum("tgd,gcd->tgc", partial_blocks, enc_blocks).astype(jnp.bfloat16)
        piece_code = lax.optimization_barrier(piece_code)
        codes = codes + piece_code.astype(jnp.float32)
        enc_term = enc_term + jnp.einsum("tgc,tgd->gcd", grad_wide, partial_blocks)
        return (codes, enc_term), None

    starting = (jnp.zeros((TOKENS, GROUPS, group_code), jnp.float32), jnp.zeros((GROUPS, group_code, group_feat), jnp.float32))
    (codes, enc_term), _ = lax.scan(accumulate, starting, jnp.arange(N_TENSOR, dtype=jnp.int32))
    code = codes.astype(jnp.bfloat16)
    code = lax.optimization_barrier(code)
    code_wide = code.astype(jnp.float32)
    layer_out = jnp.einsum("tgc,gcd->tgd", code_wide, dec_blocks).reshape(TOKENS, D).astype(jnp.bfloat16)
    decoder_grad = jnp.einsum("tgc,tgd->gcd", code_wide, cot_blocks).reshape(C, group_feat)
    encoder_grad = enc_term.reshape(C, group_feat)
    projected_grad = jnp.einsum("tgc,gcd->tgd", grad_wide, enc_blocks).reshape(TOKENS, D).astype(jnp.bfloat16)
    context_grad = lax.dot_general(projected_grad, w_out, (((1,), (1,)), ((), ())), preferred_element_type=jnp.float32).astype(jnp.bfloat16)
    w_out_grad = data_groups(context, projected_grad)
    return layer_out, context_grad, w_out_grad, encoder_grad, decoder_grad
```

```python
import jax
import jax.numpy as jnp
from jax import lax
from jax.experimental import pallas as pl
from jax.experimental.pallas import tpu as pltpu
from jax.sharding import PartitionSpec as P

GROUPS = 16
BF = jnp.bfloat16
F32 = jnp.float32
MIB = 1024 * 1024

TENSOR_RELS = [(dz, dx, dc) for dz in range(2) for dx in range(4) for dc in range(2)]
DP_RELS = [(dy, dz) for dy in range(4) for dz in range(4)]


def tensor_add(t, rel, sign=1):
    dz, dx, dc = rel
    zh, x, c = t // 8, (t // 2) % 4, t % 2
    return ((zh + 2 + sign * dz) % 2) * 8 + ((x + 4 + sign * dx) % 4) * 2 + (c + 2 + sign * dc) % 2


def dp_add(i, rel, sign=1):
    dy, dz = rel
    y, zl = i // 4, i % 4
    return ((y + 4 + sign * dy) % 4) * 4 + (zl + 4 + sign * dz) % 4


def send_tensor(v, rel):
    return lax.ppermute(v, "tensor", [(s, tensor_add(s, rel)) for s in range(16)])


def fetch_tensor(v, rel):
    return lax.ppermute(v, "tensor", [(s, tensor_add(s, rel, -1)) for s in range(16)])


def send_dp(v, rel):
    return lax.ppermute(v, "dp", [(s, dp_add(s, rel)) for s in range(16)])


def tadd(t, rel):
    dz, dx, dc = rel
    zh, x, c = t // 8, lax.rem(t // 2, 4), lax.rem(t, 2)
    return lax.rem(zh + dz, 2) * 8 + lax.rem(x + dx, 4) * 2 + lax.rem(c + dc, 2)


def dadd(i, rel):
    dy, dz = rel
    y, zl = i // 4, lax.rem(i, 4)
    return lax.rem(y + dy, 4) * 4 + lax.rem(zl + dz, 4)


def ds(start, size):
    return pl.ds(pl.multiple_of(start * size, size), size)


def dot(a, b, dims):
    return lax.dot_general(a, b, (dims, ((), ())), preferred_element_type=F32)


def params(mib):
    return pltpu.CompilerParams(vmem_limit_bytes=mib * MIB)


def cost(flops, nbytes):
    return pl.CostEstimate(flops=flops, bytes_accessed=nbytes, transcendentals=0)


def vmem(n):
    return [pl.BlockSpec(memory_space=pltpu.VMEM)] * n


def shape(*dims, dtype=BF):
    return jax.ShapeDtypeStruct(dims, dtype)


def grad_code_kernel(cot, dec, out):
    for g in range(GROUPS):
        out[:, g * 128:(g + 1) * 128] = dot(
            cot[:, g * 384:(g + 1) * 384], dec[g * 128:(g + 1) * 128, :], ((1,), (1,))
        ).astype(BF)


def cot_pieces_kernel(cot, *outs):
    i = lax.axis_index("dp")
    for out, rel in zip(outs, DP_RELS):
        out[...] = cot[:, ds(dadd(i, rel), 384)]


def encode_kernel(ctx, w, enc, own, other, wenc, ctx_t, ctx_r):
    t = lax.axis_index("tensor")

    @pl.when(pl.program_id(0) == 0)
    def _():
        n = 0
        for dc in range(2):
            for dx in range(4):
                for dz in range(2):
                    ctx_r[n * 32:(n + 1) * 32, :] = ctx[ds(tadd(t, (dz, dx, dc)), 32), :]
                    n += 1
        ctx_t[...] = ctx[...].T

    for u in range(2):
        wenc[:, u * 128:(u + 1) * 128] = dot(
            w[:, u * 384:(u + 1) * 384], enc[u * 128:(u + 1) * 128, :], ((1,), (1,))
        ).astype(BF)
    coded = dot(ctx_r[...], wenc[...], ((1,), (0,))).astype(BF)
    own[...] = coded[:256]
    other[...] = coded[256:]


def encode(ctx, w, enc):
    return pl.pallas_call(
        encode_kernel,
        grid=(8,),
        in_specs=[
            pl.BlockSpec((512, 384), lambda s: (0, 0)),
            pl.BlockSpec((384, 768), lambda s: (0, s)),
            pl.BlockSpec((256, 384), lambda s: (s, 0)),
        ],
        out_specs=[
            pl.BlockSpec((256, 256), lambda s: (0, s)),
            pl.BlockSpec((256, 256), lambda s: (0, s)),
            pl.BlockSpec((384, 256), lambda s: (0, s)),
            pl.BlockSpec((384, 512), lambda s: (0, 0)),
        ],
        out_shape=[shape(256, 2048), shape(256, 2048), shape(384, 2048), shape(384, 512)],
        scratch_shapes=[pltpu.VMEM((512, 384), BF)],
        compiler_params=params(12),
        cost_estimate=cost(1_400_000_000, 10 * MIB),
        name="encode",
    )(ctx, w, enc)


def gather_rows(pieces, whole):
    t = lax.axis_index("tensor")
    for piece, rel in zip(pieces, TENSOR_RELS):
        whole[ds(tadd(t, rel), 32), :] = piece[...]


def moment_kernel(*refs):
    pieces, ctx_t, outs, whole = refs[:16], refs[16], refs[17:21], refs[21]
    gather_rows(pieces, whole)
    i = lax.axis_index("dp")
    for dy in range(4):
        cols = jnp.concatenate(
            [whole[:, ds(dadd(i, (dy, dz)), 128)] for dz in range(4)], axis=1
        )
        outs[dy][...] = dot(ctx_t[...], cols, ((1,), (0,))).astype(BF)


def moment(pieces, ctx_t):
    return pl.pallas_call(
        moment_kernel,
        in_specs=vmem(17),
        out_specs=vmem(4),
        out_shape=[shape(384, 512)] * 4,
        scratch_shapes=[pltpu.VMEM((512, 2048), BF)],
        compiler_params=params(16),
        cost_estimate=cost(805_000_000, 4 * MIB),
        name="moment",
    )(*pieces, ctx_t)


def context_grad_kernel(*refs):
    pieces, wenc, out, whole = refs[:16], refs[16], refs[17], refs[18]
    gather_rows(pieces, whole)
    out[...] = dot(whole[...], wenc[...], ((1,), (1,))).astype(BF)


def context_grad_of(pieces, wenc):
    return pl.pallas_call(
        context_grad_kernel,
        in_specs=vmem(17),
        out_specs=vmem(1)[0],
        out_shape=shape(512, 384),
        scratch_shapes=[pltpu.VMEM((512, 2048), BF)],
        compiler_params=params(16),
        cost_estimate=cost(805_000_000, 4 * MIB),
        name="context_grad",
    )(*pieces, wenc)


def code_kernel(own, recv, code, *outs):
    code[...] = (own[...].astype(F32) + recv[...].astype(F32)).astype(BF)
    i = lax.axis_index("dp")
    for out, rel in zip(outs, DP_RELS):
        out[...] = code[:, ds(dadd(i, rel), 128)]


def layer_out_kernel(code, dec, out):
    for g in range(GROUPS):
        out[:, g * 384:(g + 1) * 384] = dot(
            code[:, g * 128:(g + 1) * 128], dec[g * 128:(g + 1) * 128, :], ((1,), (0,))
        ).astype(BF)


def spread_rows(term, outs):
    t = lax.axis_index("tensor")
    for out, rel in zip(outs, TENSOR_RELS):
        out[...] = term[ds(tadd(t, rel), 8), :]


def decoder_grad_kernel(*refs):
    codes, cots, outs, term = refs[:16], refs[16:32], refs[32:48], refs[48]
    code = jnp.concatenate([r[...] for r in codes], axis=0)
    cot = jnp.concatenate([r[...] for r in cots], axis=0)
    term[...] = dot(code, cot, ((0,), (0,)))
    spread_rows(term, outs)


def encoder_grad_kernel(w_hbm, *refs):
    parts, total, outs, term, w_block, sem = refs[:4], refs[4], refs[5:21], refs[21], refs[22], refs[23]
    i = lax.axis_index("dp")
    copy = pltpu.make_async_copy(w_hbm.at[:, ds(i, 384)], w_block, sem)
    copy.start()
    total[...] = sum(r[...].astype(F32) for r in parts).astype(BF)
    copy.wait()
    term[...] = dot(total[...], w_block[...], ((0,), (0,)))
    spread_rows(term, outs)


def w_out_grad_kernel(total, enc, out):
    i = lax.axis_index("dp")
    out[...] = dot(total[...], enc[ds(i, 128), :], ((1,), (0,)))


def add(*parts):
    return sum(p.astype(F32) for p in parts)


def on_device(ctx, w, enc, dec, cot):
    grad_code = pl.pallas_call(
        grad_code_kernel,
        in_specs=vmem(2),
        out_specs=vmem(1)[0],
        out_shape=shape(32, 2048),
        compiler_params=params(8),
        cost_estimate=cost(50_000_000, 2 * MIB),
        name="grad_code",
    )(cot, dec)

    pieces = {(0, 0, 0): grad_code}
    for dx in (2, 1, 3):
        pieces[0, dx, 0] = fetch_tensor(grad_code, (0, dx, 0))
    pieces[1, 0, 0] = fetch_tensor(grad_code, (1, 0, 0))
    for dx in (2, 1, 3):
        pieces[1, dx, 0] = fetch_tensor(pieces[1, 0, 0], (0, dx, 0))
    for dz in range(2):
        for dx in range(4):
            pieces[dz, dx, 1] = fetch_tensor(pieces[dz, dx, 0], (0, 0, 1))
    pieces = [pieces[rel] for rel in TENSOR_RELS]

    cots = pl.pallas_call(
        cot_pieces_kernel,
        in_specs=vmem(1),
        out_specs=vmem(16),
        out_shape=[shape(32, 384)] * 16,
        compiler_params=params(4),
        cost_estimate=cost(0, 1 * MIB),
        name="cot_pieces",
    )(cot)
    cots = [v if rel == (0, 0) else send_dp(v, rel) for v, rel in zip(cots, DP_RELS)]

    own, other, wenc, ctx_t = encode(ctx, w, enc)
    got = send_tensor(other, (0, 0, 1))
    part = [add(own[64 * k:64 * k + 64], got[64 * k:64 * k + 64]).astype(BF) for k in range(4)]
    rows = [part[0]] + [send_tensor(part[k], (0, k, 0)) for k in (2, 1, 3)]
    far = add(*[r[32:] for r in rows]).astype(BF)
    near = add(*[r[:32] for r in rows]).astype(BF)
    got = send_tensor(far, (1, 0, 0))
    code, *codes = pl.pallas_call(
        code_kernel,
        in_specs=vmem(2),
        out_specs=vmem(17),
        out_shape=[shape(32, 2048)] + [shape(32, 128)] * 16,
        compiler_params=params(4),
        cost_estimate=cost(0, 1 * MIB),
        name="code",
    )(near, got)
    codes = [v if rel == (0, 0) else send_dp(v, rel) for v, rel in zip(codes, DP_RELS)]

    chunks = moment(pieces, ctx_t)
    chunks = [chunks[0]] + [send_dp(chunks[k], (k, 0)) for k in (2, 1, 3)]
    subs = [
        add(*[c[:, 128 * k:128 * k + 128] for c in chunks]).astype(BF) for k in range(4)
    ]
    subs = [subs[0]] + [send_dp(subs[k], (0, k)) for k in (2, 1, 3)]

    context_grad = context_grad_of(pieces, wenc)
    layer_out = pl.pallas_call(
        layer_out_kernel,
        in_specs=vmem(2),
        out_specs=vmem(1)[0],
        out_shape=shape(32, 6144),
        compiler_params=params(8),
        cost_estimate=cost(50_000_000, 2 * MIB),
        name="layer_out",
    )(code, dec)

    terms = pl.pallas_call(
        decoder_grad_kernel,
        in_specs=vmem(32),
        out_specs=vmem(16),
        out_shape=[shape(8, 384, dtype=F32)] * 16,
        scratch_shapes=[pltpu.VMEM((128, 384), F32)],
        compiler_params=params(8),
        cost_estimate=cost(50_000_000, 1 * MIB),
        name="decoder_grad",
    )(*codes, *cots)
    decoder_grad = add(*[
        v if rel == (0, 0, 0) else send_tensor(v, rel) for v, rel in zip(terms, TENSOR_RELS)
    ])

    total, *terms = pl.pallas_call(
        encoder_grad_kernel,
        in_specs=[pl.BlockSpec(memory_space=pl.ANY)] + vmem(4),
        out_specs=vmem(17),
        out_shape=[shape(384, 128)] + [shape(8, 384, dtype=F32)] * 16,
        scratch_shapes=[
            pltpu.VMEM((128, 384), F32), pltpu.VMEM((384, 384), BF), pltpu.SemaphoreType.DMA,
        ],
        compiler_params=params(8),
        cost_estimate=cost(50_000_000, 1 * MIB),
        name="encoder_grad",
    )(w, *subs)
    encoder_grad = add(*[
        v if rel == (0, 0, 0) else send_tensor(v, rel) for v, rel in zip(terms, TENSOR_RELS)
    ])
    w_out_grad = pl.pallas_call(
        w_out_grad_kernel,
        in_specs=vmem(2),
        out_specs=vmem(1)[0],
        out_shape=shape(384, 384, dtype=F32),
        compiler_params=params(8),
        cost_estimate=cost(50_000_000, 2 * MIB),
        name="w_out_grad",
    )(total, enc)
    return layer_out, context_grad, w_out_grad, encoder_grad, decoder_grad


def solution(mesh):
    placed = (P("dp", "tensor"), P("tensor", None), P(), P(), P(("dp", "tensor"), None))
    return jax.shard_map(
        on_device,
        mesh=mesh,
        in_specs=placed,
        out_specs=(
            P(("dp", "tensor"), None),
            P("dp", "tensor"),
            P("tensor", "dp"),
            P(("dp", "tensor"), None),
            P(("dp", "tensor"), None),
        ),
        check_vma=False,
    )
```

```python
import jax
import jax.numpy as jnp
from jax import lax
from jax.experimental import pallas as pl
from jax.experimental.pallas import tpu as pltpu
from jax.sharding import PartitionSpec as P

GROUPS = 16
BF = jnp.bfloat16
F32 = jnp.float32
MIB = 1024 * 1024
FIRST_VMEM = 125 * MIB // 2

TENSOR_RELS = [(dz, dx, dc) for dz in range(2) for dx in range(4) for dc in range(2)]


def tensor_add(t, rel, sign=1):
    dz, dx, dc = rel
    zh, x, c = t // 8, (t // 2) % 4, t % 2
    return ((zh + 2 + sign * dz) % 2) * 8 + ((x + 4 + sign * dx) % 4) * 2 + (c + 2 + sign * dc) % 2


def dp_add(i, rel, sign=1):
    dy, dz = rel
    y, zl = i // 4, i % 4
    return ((y + 4 + sign * dy) % 4) * 4 + (zl + 4 + sign * dz) % 4


def send_tensor(v, rel):
    return lax.ppermute(v, "tensor", [(s, tensor_add(s, rel)) for s in range(16)])


def fetch_tensor(v, rel):
    return lax.ppermute(v, "tensor", [(s, tensor_add(s, rel, -1)) for s in range(16)])


def swap_x(v, r):
    return lax.ppermute(v, "tensor", [(s, s ^ (2 * r)) for s in range(16)])


def swap_y(v, r):
    return lax.ppermute(v, "dp", [(s, s ^ (4 * r)) for s in range(16)])


def send_dp(v, rel):
    return lax.ppermute(v, "dp", [(s, dp_add(s, rel)) for s in range(16)])


def tadd(t, rel):
    dz, dx, dc = rel
    zh, x, c = t // 8, lax.rem(t // 2, 4), lax.rem(t, 2)
    return lax.rem(zh + dz, 2) * 8 + lax.rem(x + dx, 4) * 2 + lax.rem(c + dc, 2)


def dadd(i, rel):
    dy, dz = rel
    y, zl = i // 4, lax.rem(i, 4)
    return lax.rem(y + dy, 4) * 4 + lax.rem(zl + dz, 4)


def ds(start, size):
    return pl.ds(pl.multiple_of(start * size, size), size)


def dot(a, b, dims):
    return lax.dot_general(a, b, (dims, ((), ())), preferred_element_type=F32)


def params(mib):
    return pltpu.CompilerParams(vmem_limit_bytes=mib * MIB)


def cost(flops, nbytes):
    return pl.CostEstimate(flops=flops, bytes_accessed=nbytes, transcendentals=0)


def vmem(n):
    return [pl.BlockSpec(memory_space=pltpu.VMEM)] * n


def shape(*dims, dtype=BF):
    return jax.ShapeDtypeStruct(dims, dtype)


def grad_code_kernel(cot_hbm, dec_hbm, out, *rest):
    chunks, (cot, dec, sems) = rest[:4], rest[4:]
    copies = [pltpu.make_async_copy(cot_hbm, cot, sems.at[4])] + [
        pltpu.make_async_copy(
            dec_hbm.at[k * 512:(k + 1) * 512, :], dec.at[k * 512:(k + 1) * 512, :], sems.at[k]
        )
        for k in range(4)
    ]
    for copy in copies:
        copy.start()
    copies[0].wait()
    by_group(cot, 384, chunks)
    for g in range(GROUPS):
        if g % 4 == 0:
            copies[1 + g // 4].wait()
        out[:, g * 128:(g + 1) * 128] = dot(
            cot[:, g * 384:(g + 1) * 384], dec[g * 128:(g + 1) * 128, :], ((1,), (1,))
        ).astype(BF)


def any_space(n):
    return [pl.BlockSpec(memory_space=pl.ANY)] * n


def by_group(source, width, outs):
    i = lax.axis_index("dp")
    for dy in range(4):
        for dz in range(4):
            outs[dy][:, dz * width:(dz + 1) * width] = source[:, ds(dadd(i, (dy, dz)), width)]


def regroup(blocks, outs):
    n = outs[0].shape[1]
    for k in range(4):
        for b in range(4):
            outs[k][b * 32:(b + 1) * 32, :] = blocks[b][:, k * n:(k + 1) * n]


def code_regroup_kernel(*refs):
    regroup(refs[:4], refs[4:])


def code_regroup(blocks):
    return pl.pallas_call(
        code_regroup_kernel,
        in_specs=vmem(4),
        out_specs=vmem(4),
        out_shape=[shape(128, 128)] * 4,
        compiler_params=params(4),
        cost_estimate=cost(0, MIB // 4),
        name="code_regroup",
    )(*blocks)


def over_y(chunks):
    return [chunks[0]] + [send_dp(chunks[k], (k, 0)) for k in (1, 2, 3)]


def over_z(chunks):
    return [chunks[0]] + [send_dp(chunks[k], (0, k)) for k in (1, 2, 3)]


def wenc_kernel(w_hbm, ctx, enc, after, wenc, ctx_t, ctx_r, w, sems):
    copies = [
        pltpu.make_async_copy(
            w_hbm.at[:, k * 1536:(k + 1) * 1536], w.at[:, k * 1536:(k + 1) * 1536], sems.at[k]
        )
        for k in range(4)
    ]
    for copy in copies:
        copy.start()
    t = lax.axis_index("tensor")
    zh, x, c = t // 8, lax.rem(t // 2, 4), lax.rem(t, 2)
    n = 0
    for dc in range(2):
        for dz, order in ((1, (1, 2, 0, 3)), (0, (3, 2, 0, 1))):
            for r in order:
                chunk = lax.rem(zh + dz, 2) * 8 + (x ^ r) * 2 + lax.rem(c + dc, 2)
                ctx_r[n * 32:(n + 1) * 32, :] = ctx[ds(chunk, 32), :]
                n += 1
    ctx_t[...] = ctx[...].T
    for g in range(GROUPS):
        if g % 4 == 0:
            copies[g // 4].wait()
        wenc[:, g * 128:(g + 1) * 128] = dot(
            w[:, g * 384:(g + 1) * 384], enc[g * 128:(g + 1) * 128, :], ((1,), (1,))
        ).astype(BF)


def wenc_of(w, ctx, enc, after):
    return pl.pallas_call(
        wenc_kernel,
        in_specs=[pl.BlockSpec(memory_space=pltpu.HBM)] + vmem(2) + any_space(1),
        out_specs=vmem(3),
        out_shape=[shape(384, 2048), shape(384, 512), shape(512, 384)],
        scratch_shapes=[pltpu.VMEM((384, 6144), BF), pltpu.SemaphoreType.DMA((4,))],
        compiler_params=params(16),
        cost_estimate=cost(604_000_000, 9 * MIB),
        name="wenc",
    )(w, ctx, enc, after)


def coded_kernel(*refs):
    ctx_r, wenc, mine, theirs, blocks = refs[0], refs[1], refs[2], refs[3], refs[4:8]
    own, other, pair, chunks = refs[8], refs[9], refs[10], refs[11:]
    pair[:32, :] = mine[...]
    pair[32:, :] = theirs[...]
    regroup(blocks, chunks)
    for k in range(4):
        cols = slice(k * 512, (k + 1) * 512)
        coded = dot(ctx_r[...], wenc[:, cols], ((1,), (0,))).astype(BF)
        own[:, cols] = coded[:256]
        other[:, cols] = coded[256:]


def coded_of(ctx_r, wenc, mine, theirs, blocks):
    return pl.pallas_call(
        coded_kernel,
        in_specs=vmem(8),
        out_specs=vmem(7),
        out_shape=[shape(256, 2048)] * 2 + [shape(64, 2048)] + [shape(128, 384)] * 4,
        compiler_params=params(16),
        cost_estimate=cost(805_000_000, 4 * MIB),
        name="coded",
    )(ctx_r, wenc, mine, theirs, *blocks)


def pack_kernel(*refs):
    pieces, own, got, packed, outs = refs[:4], refs[4], refs[5], refs[-5], refs[-4:]
    for k in range(4):
        packed[k * 64:(k + 1) * 64, :] = pieces[k][...]
    for k in range(4):
        rows = slice(k * 64, (k + 1) * 64)
        outs[k][...] = (own[rows, :].astype(F32) + got[rows, :].astype(F32)).astype(BF)


def pack(pieces, own, got, *after):
    return pl.pallas_call(
        pack_kernel,
        in_specs=vmem(6) + any_space(len(after)),
        out_specs=vmem(5),
        out_shape=[shape(256, 2048)] + [shape(64, 2048)] * 4,
        compiler_params=params(12),
        cost_estimate=cost(0, 2 * MIB),
        name="pack",
    )(*pieces, own, got, *after)


def gather_rows(near, far, whole):
    t = lax.axis_index("tensor")
    for dc, half in enumerate((near, far)):
        for dx in range(4):
            for dz in range(2):
                n = dx * 64 + dz * 32
                whole[ds(tadd(t, (dz, dx, dc)), 32), :] = half[n:n + 32, :]


def moment_kernel(near, far, ctx_t, a_send, a_keep, b_send, b_keep, whole):
    gather_rows(near, far, whole)
    i = lax.axis_index("dp")
    y, zl = i // 4, lax.rem(i, 4)
    places = {
        1: ((a_send, 0), (b_keep, 1)),
        2: ((a_send, 1), (b_send, 1)),
        3: ((a_keep, 1), (b_send, 0)),
        0: ((a_keep, 0), (b_keep, 0)),
    }
    for r, halves in places.items():
        cols = jnp.concatenate(
            [whole[:, ds((y ^ r) * 4 + lax.rem(zl + dz, 4), 128)] for dz in range(4)], axis=1
        )
        out = dot(ctx_t[...], cols, ((1,), (0,))).astype(BF)
        for h, (ref, n) in enumerate(halves):
            ref[n * 384:(n + 1) * 384, :] = out[:, h * 256:(h + 1) * 256]


def moment(near, far, ctx_t):
    return pl.pallas_call(
        moment_kernel,
        in_specs=vmem(3),
        out_specs=vmem(4),
        out_shape=[shape(768, 256)] * 4,
        scratch_shapes=[pltpu.VMEM((512, 2048), BF)],
        compiler_params=params(16),
        cost_estimate=cost(805_000_000, 4 * MIB),
        name="moment",
    )(near, far, ctx_t)


def context_grad_kernel(*refs):
    near, far, wenc, out, whole = refs[0], refs[1], refs[2], refs[-2], refs[-1]
    gather_rows(near, far, whole)
    out[...] = dot(whole[...], wenc[...], ((1,), (1,))).astype(BF)


def context_grad_of(near, far, wenc):
    return pl.pallas_call(
        context_grad_kernel,
        in_specs=vmem(3),
        out_specs=vmem(1)[0],
        out_shape=shape(512, 384),
        scratch_shapes=[pltpu.VMEM((512, 2048), BF)],
        compiler_params=params(16),
        cost_estimate=cost(805_000_000, 4 * MIB),
        name="context_grad",
    )(near, far, wenc)


def add_refs(*parts):
    return sum(p.astype(F32) for p in parts)


def second_x_kernel(a_keep, a_got, b_keep, b_got, after, a_send, b_send):
    a_send[...] = add_refs(a_keep[32:, :], a_got[32:, :]).astype(BF)
    b_send[...] = add_refs(b_keep[32:, :], b_got[32:, :]).astype(BF)


def second_x(a_keep, a_got, b_keep, b_got, after):
    return pl.pallas_call(
        second_x_kernel,
        in_specs=vmem(4) + any_space(1),
        out_specs=vmem(2),
        out_shape=[shape(32, 2048)] * 2,
        compiler_params=params(4),
        cost_estimate=cost(0, 1 * MIB),
        name="second_x",
    )(a_keep, a_got, b_keep, b_got, after)


def second_y_kernel(*refs):
    a_keep, a_got, a_last, b_keep, b_got, b_last = refs[:6]
    ma_keep, ma_got, mb_keep, mb_got, far, near, a_send, b_send = refs[6:]
    far[...] = add_refs(a_keep[:32, :], a_got[:32, :], a_last[...]).astype(BF)
    near[...] = add_refs(b_keep[:32, :], b_got[:32, :], b_last[...])
    a_send[...] = add_refs(ma_keep[384:, :], ma_got[384:, :]).astype(BF)
    b_send[...] = add_refs(mb_keep[384:, :], mb_got[384:, :]).astype(BF)


def second_y(*parts):
    return pl.pallas_call(
        second_y_kernel,
        in_specs=vmem(10),
        out_specs=vmem(4),
        out_shape=[shape(32, 2048), shape(32, 2048, dtype=F32)] + [shape(384, 256)] * 2,
        compiler_params=params(8),
        cost_estimate=cost(0, 2 * MIB),
        name="second_y",
    )(*parts)


def moment_sum_kernel(a_keep, a_got, a_last, b_keep, b_got, b_last, *outs):
    for n, refs in enumerate(((a_keep, a_got, a_last), (b_keep, b_got, b_last))):
        total = add_refs(refs[0][:384, :], refs[1][:384, :], refs[2][...]).astype(BF)
        outs[2 * n][...] = total[:, :128]
        outs[2 * n + 1][...] = total[:, 128:]


def moment_sum(*parts):
    return pl.pallas_call(
        moment_sum_kernel,
        in_specs=vmem(6),
        out_specs=vmem(4),
        out_shape=[shape(384, 128)] * 4,
        compiler_params=params(8),
        cost_estimate=cost(0, 2 * MIB),
        name="moment_sum",
    )(*parts)


def code_kernel(near, recv, after, code, *outs):
    code[...] = (near[...] + recv[...].astype(F32)).astype(BF)
    by_group(code, 128, outs)


def code_of(near, recv, after):
    return pl.pallas_call(
        code_kernel,
        in_specs=vmem(2) + any_space(1),
        out_specs=vmem(5),
        out_shape=[shape(32, 2048)] + [shape(32, 512)] * 4,
        compiler_params=params(8),
        cost_estimate=cost(0, 1 * MIB),
        name="code",
    )(near, recv, after)


def layer_out_kernel(code, dec, out):
    for g in range(GROUPS):
        out[:, g * 384:(g + 1) * 384] = dot(
            code[:, g * 128:(g + 1) * 128], dec[g * 128:(g + 1) * 128, :], ((1,), (0,))
        ).astype(BF)


def codec_grads_kernel(w_hbm, *refs):
    parts, codes, cots = refs[:4], refs[4:8], refs[8:12]
    total, own, other, enc_term, dec_term, w_block, sem = refs[12:]
    i, t = lax.axis_index("dp"), lax.axis_index("tensor")
    copy = pltpu.make_async_copy(w_hbm.at[:, ds(i, 384)], w_block, sem)
    copy.start()
    code = jnp.concatenate([r[...] for r in codes], axis=0)
    cot = jnp.concatenate([r[...] for r in cots], axis=0)
    dec_term[...] = dot(code, cot, ((0,), (0,)))
    total[...] = sum(r[...].astype(F32) for r in parts).astype(BF)
    copy.wait()
    enc_term[...] = dot(total[...], w_block[...], ((0,), (0,)))
    for dc, out in enumerate((own, other)):
        n = 0
        for dx in range(4):
            for dz in range(2):
                rows = ds(tadd(t, (dz, dx, dc)), 8)
                out[n:n + 8, :] = enc_term[rows, :]
                out[n + 8:n + 16, :] = dec_term[rows, :]
                n += 16


def w_out_grad_kernel(total, enc, out):
    i = lax.axis_index("dp")
    out[...] = dot(total[...], enc[ds(i, 128), :], ((1,), (0,)))


def add(*parts):
    return sum(p.astype(F32) for p in parts)


def on_device(ctx, w, enc, dec, cot):
    grad_code, *cots = pl.pallas_call(
        grad_code_kernel,
        in_specs=[pl.BlockSpec(memory_space=pltpu.HBM)] * 2,
        out_specs=vmem(5),
        out_shape=[shape(32, 2048)] + [shape(32, 1536)] * 4,
        scratch_shapes=[
            pltpu.VMEM((32, 6144), BF), pltpu.VMEM((2048, 384), BF),
            pltpu.SemaphoreType.DMA((5,)),
        ],
        compiler_params=pltpu.CompilerParams(vmem_limit_bytes=FIRST_VMEM),
        cost_estimate=cost(50_000_000, 2 * MIB),
        name="grad_code",
    )(cot, dec)

    theirs = fetch_tensor(grad_code, (1, 0, 0))
    cots = over_y(cots)
    wenc, ctx_t, ctx_r = wenc_of(w, ctx, enc, cots[1])

    own, other, pair, *cots = coded_of(ctx_r, wenc, grad_code, theirs, cots)
    pieces = [pair] + [fetch_tensor(pair, (0, k, 0)) for k in (1, 2, 3)]
    got = send_tensor(other, (0, 0, 1))
    cots = over_z(cots)

    packed, a_send, a_keep, b_send, b_keep = pack(pieces, own, got, *cots[1:])
    packed_far = send_tensor(packed, (0, 0, 1))
    a_got, b_got = swap_x(a_send, 1), swap_x(b_send, 3)

    ma_send, ma_keep, mb_send, mb_keep = moment(packed, packed_far, ctx_t)
    ma_got, mb_got = swap_y(ma_send, 1), swap_y(mb_send, 3)

    a_send, b_send = second_x(a_keep, a_got, b_keep, b_got, ma_send)
    a_last, b_last = swap_x(a_send, 3), swap_x(b_send, 1)

    far, near, a_send, b_send = second_y(
        a_keep, a_got, a_last, b_keep, b_got, b_last, ma_keep, ma_got, mb_keep, mb_got
    )
    recv = send_tensor(far, (1, 0, 0))
    ma_last, mb_last = swap_y(a_send, 3), swap_y(b_send, 1)

    subs = over_z(moment_sum(ma_keep, ma_got, ma_last, mb_keep, mb_got, mb_last))
    code, *codes = code_of(near, recv, subs[1])
    codes = over_z(code_regroup(over_y(codes)))

    context_grad = context_grad_of(packed, packed_far, wenc)
    layer_out = pl.pallas_call(
        layer_out_kernel,
        in_specs=vmem(2),
        out_specs=vmem(1)[0],
        out_shape=shape(32, 6144),
        compiler_params=params(8),
        cost_estimate=cost(50_000_000, 2 * MIB),
        name="layer_out",
    )(code, dec)

    total, own, other = pl.pallas_call(
        codec_grads_kernel,
        in_specs=[pl.BlockSpec(memory_space=pltpu.HBM)] + vmem(12),
        out_specs=vmem(3),
        out_shape=[shape(384, 128)] + [shape(128, 384, dtype=F32)] * 2,
        scratch_shapes=[
            pltpu.VMEM((128, 384), F32), pltpu.VMEM((128, 384), F32),
            pltpu.VMEM((384, 384), BF), pltpu.SemaphoreType.DMA,
        ],
        compiler_params=params(8),
        cost_estimate=cost(100_000_000, 2 * MIB),
        name="codec_grads",
    )(w, *subs, *codes, *cots)
    got = send_tensor(other, (0, 0, 1))
    part = [add(own[32 * k:32 * k + 32], got[32 * k:32 * k + 32]) for k in range(4)]
    rows = [part[0]] + [send_tensor(part[k], (0, k, 0)) for k in (2, 1, 3)]
    far = add(*[r[16:] for r in rows])
    near = add(*[r[:16] for r in rows])
    grads = near + send_tensor(far, (1, 0, 0))
    encoder_grad, decoder_grad = grads[:8], grads[8:]
    w_out_grad = pl.pallas_call(
        w_out_grad_kernel,
        in_specs=vmem(2),
        out_specs=vmem(1)[0],
        out_shape=shape(384, 384, dtype=F32),
        compiler_params=params(8),
        cost_estimate=cost(50_000_000, 2 * MIB),
        name="w_out_grad",
    )(total, enc)
    return layer_out, context_grad, w_out_grad, encoder_grad, decoder_grad


def solution(mesh):
    placed = (P("dp", "tensor"), P("tensor", None), P(), P(), P(("dp", "tensor"), None))
    return jax.shard_map(
        on_device,
        mesh=mesh,
        in_specs=placed,
        out_specs=(
            P(("dp", "tensor"), None),
            P("dp", "tensor"),
            P("tensor", "dp"),
            P(("dp", "tensor"), None),
            P(("dp", "tensor"), None),
        ),
        check_vma=False,
    )
```

```python
import jax
import jax.numpy as jnp
from jax import lax
from jax.experimental import pallas as pl
from jax.experimental.pallas import tpu as pltpu
from jax.sharding import PartitionSpec as P

GROUPS = 16
BF = jnp.bfloat16
F32 = jnp.float32
MIB = 1024 * 1024
FIRST_VMEM = 60 * MIB

TENSOR_RELS = [(dz, dx, dc) for dz in range(2) for dx in range(4) for dc in range(2)]


def tensor_add(t, rel, sign=1):
    dz, dx, dc = rel
    zh, x, c = t // 8, (t // 2) % 4, t % 2
    return ((zh + 2 + sign * dz) % 2) * 8 + ((x + 4 + sign * dx) % 4) * 2 + (c + 2 + sign * dc) % 2


def dp_add(i, rel, sign=1):
    dy, dz = rel
    y, zl = i // 4, i % 4
    return ((y + 4 + sign * dy) % 4) * 4 + (zl + 4 + sign * dz) % 4


def send_tensor(v, rel):
    return lax.ppermute(v, "tensor", [(s, tensor_add(s, rel)) for s in range(16)])


def fetch_tensor(v, rel):
    return lax.ppermute(v, "tensor", [(s, tensor_add(s, rel, -1)) for s in range(16)])


def swap_x(v, r):
    return lax.ppermute(v, "tensor", [(s, s ^ (2 * r)) for s in range(16)])


def swap_y(v, r):
    return lax.ppermute(v, "dp", [(s, s ^ (4 * r)) for s in range(16)])


def send_dp(v, rel):
    return lax.ppermute(v, "dp", [(s, dp_add(s, rel)) for s in range(16)])


def tadd(t, rel):
    dz, dx, dc = rel
    zh, x, c = t // 8, lax.rem(t // 2, 4), lax.rem(t, 2)
    return lax.rem(zh + dz, 2) * 8 + lax.rem(x + dx, 4) * 2 + lax.rem(c + dc, 2)


def dadd(i, rel):
    dy, dz = rel
    y, zl = i // 4, lax.rem(i, 4)
    return lax.rem(y + dy, 4) * 4 + lax.rem(zl + dz, 4)


def ds(start, size):
    return pl.ds(pl.multiple_of(start * size, size), size)


def dot(a, b, dims):
    return lax.dot_general(a, b, (dims, ((), ())), preferred_element_type=F32)


def params(mib):
    return pltpu.CompilerParams(vmem_limit_bytes=mib * MIB)


def cost(flops, nbytes):
    return pl.CostEstimate(flops=flops, bytes_accessed=nbytes, transcendentals=0)


def vmem(n):
    return [pl.BlockSpec(memory_space=pltpu.VMEM)] * n


def shape(*dims, dtype=BF):
    return jax.ShapeDtypeStruct(dims, dtype)


def grad_code_kernel(cot_hbm, dec_hbm, out, *rest):
    chunks, (cot, dec, sems) = rest[:4], rest[4:]
    copies = [pltpu.make_async_copy(cot_hbm, cot, sems.at[4])] + [
        pltpu.make_async_copy(
            dec_hbm.at[k * 512:(k + 1) * 512, :], dec.at[k * 512:(k + 1) * 512, :], sems.at[k]
        )
        for k in range(4)
    ]
    for copy in copies:
        copy.start()
    copies[0].wait()
    by_group(cot, 384, chunks)
    for g in range(GROUPS):
        if g % 4 == 0:
            copies[1 + g // 4].wait()
        out[:, g * 128:(g + 1) * 128] = dot(
            cot[:, g * 384:(g + 1) * 384], dec[g * 128:(g + 1) * 128, :], ((1,), (1,))
        ).astype(BF)


def any_space(n):
    return [pl.BlockSpec(memory_space=pl.ANY)] * n


def by_group(source, width, outs):
    i = lax.axis_index("dp")
    for dy in range(4):
        for dz in range(4):
            outs[dy][:, dz * width:(dz + 1) * width] = source[:, ds(dadd(i, (dy, dz)), width)]


def regroup(blocks, outs):
    n = outs[0].shape[1]
    for k in range(4):
        for b in range(4):
            outs[k][b * 32:(b + 1) * 32, :] = blocks[b][:, k * n:(k + 1) * n]


def code_regroup_kernel(*refs):
    regroup(refs[:4], refs[4:])


def code_regroup(blocks):
    return pl.pallas_call(
        code_regroup_kernel,
        in_specs=vmem(4),
        out_specs=vmem(4),
        out_shape=[shape(128, 128)] * 4,
        compiler_params=params(4),
        cost_estimate=cost(0, MIB // 4),
        name="code_regroup",
    )(*blocks)


def over_y(chunks):
    return [chunks[0]] + [send_dp(chunks[k], (k, 0)) for k in (1, 2, 3)]


def over_z(chunks):
    return [chunks[0]] + [send_dp(chunks[k], (0, k)) for k in (1, 2, 3)]


def wenc_kernel(w_hbm, ctx, enc, after, wenc, ctx_t, ctx_r, w, sems):
    copies = [
        pltpu.make_async_copy(
            w_hbm.at[:, k * 1536:(k + 1) * 1536], w.at[:, k * 1536:(k + 1) * 1536], sems.at[k]
        )
        for k in range(4)
    ]
    for copy in copies:
        copy.start()
    t = lax.axis_index("tensor")
    zh, x, c = t // 8, lax.rem(t // 2, 4), lax.rem(t, 2)
    n = 0
    for dc in range(2):
        for dz, order in ((1, (1, 2, 0, 3)), (0, (3, 2, 0, 1))):
            for r in order:
                chunk = lax.rem(zh + dz, 2) * 8 + (x ^ r) * 2 + lax.rem(c + dc, 2)
                ctx_r[n * 32:(n + 1) * 32, :] = ctx[ds(chunk, 32), :]
                n += 1
    ctx_t[...] = ctx[...].T
    for g in range(GROUPS):
        if g % 4 == 0:
            copies[g // 4].wait()
        wenc[:, g * 128:(g + 1) * 128] = dot(
            w[:, g * 384:(g + 1) * 384], enc[g * 128:(g + 1) * 128, :], ((1,), (1,))
        ).astype(BF)


def wenc_of(w, ctx, enc, after):
    return pl.pallas_call(
        wenc_kernel,
        in_specs=[pl.BlockSpec(memory_space=pltpu.HBM)] + vmem(2) + any_space(1),
        out_specs=vmem(3),
        out_shape=[shape(384, 2048), shape(384, 512), shape(512, 384)],
        scratch_shapes=[pltpu.VMEM((384, 6144), BF), pltpu.SemaphoreType.DMA((4,))],
        compiler_params=params(16),
        cost_estimate=cost(604_000_000, 9 * MIB),
        name="wenc",
    )(w, ctx, enc, after)


def coded_kernel(*refs):
    ctx_r, wenc, mine, theirs, blocks = refs[0], refs[1], refs[2], refs[3], refs[4:8]
    own, other, pair, chunks = refs[8], refs[9], refs[10], refs[11:]
    pair[:32, :] = mine[...]
    pair[32:, :] = theirs[...]
    regroup(blocks, chunks)
    for k in range(4):
        cols = slice(k * 512, (k + 1) * 512)
        coded = dot(ctx_r[...], wenc[:, cols], ((1,), (0,))).astype(BF)
        own[:, cols] = coded[:256]
        other[:, cols] = coded[256:]


def coded_of(ctx_r, wenc, mine, theirs, blocks):
    return pl.pallas_call(
        coded_kernel,
        in_specs=vmem(8),
        out_specs=vmem(7),
        out_shape=[shape(256, 2048)] * 2 + [shape(64, 2048)] + [shape(128, 384)] * 4,
        compiler_params=params(16),
        cost_estimate=cost(805_000_000, 4 * MIB),
        name="coded",
    )(ctx_r, wenc, mine, theirs, *blocks)


def pack_kernel(*refs):
    pieces, own, got, packed, outs = refs[:4], refs[4], refs[5], refs[-5], refs[-4:]
    for k in range(4):
        packed[k * 64:(k + 1) * 64, :] = pieces[k][...]
    for k in range(4):
        rows = slice(k * 64, (k + 1) * 64)
        outs[k][...] = (own[rows, :].astype(F32) + got[rows, :].astype(F32)).astype(BF)


def pack(pieces, own, got, *after):
    return pl.pallas_call(
        pack_kernel,
        in_specs=vmem(6) + any_space(len(after)),
        out_specs=vmem(5),
        out_shape=[shape(256, 2048)] + [shape(64, 2048)] * 4,
        compiler_params=params(12),
        cost_estimate=cost(0, 2 * MIB),
        name="pack",
    )(*pieces, own, got, *after)


def gather_rows(near, far, whole):
    t = lax.axis_index("tensor")
    for dc, half in enumerate((near, far)):
        for dx in range(4):
            for dz in range(2):
                n = dx * 64 + dz * 32
                whole[ds(tadd(t, (dz, dx, dc)), 32), :] = half[n:n + 32, :]


def moment_kernel(near, far, ctx_t, a_send, a_keep, b_send, b_keep, whole):
    gather_rows(near, far, whole)
    i = lax.axis_index("dp")
    y, zl = i // 4, lax.rem(i, 4)
    places = {
        1: ((a_send, 0), (b_keep, 1)),
        2: ((a_send, 1), (b_send, 1)),
        3: ((a_keep, 1), (b_send, 0)),
        0: ((a_keep, 0), (b_keep, 0)),
    }
    for r, halves in places.items():
        cols = jnp.concatenate(
            [whole[:, ds((y ^ r) * 4 + lax.rem(zl + dz, 4), 128)] for dz in range(4)], axis=1
        )
        out = dot(ctx_t[...], cols, ((1,), (0,))).astype(BF)
        for h, (ref, n) in enumerate(halves):
            ref[n * 384:(n + 1) * 384, :] = out[:, h * 256:(h + 1) * 256]


def moment(near, far, ctx_t):
    return pl.pallas_call(
        moment_kernel,
        in_specs=vmem(3),
        out_specs=vmem(4),
        out_shape=[shape(768, 256)] * 4,
        scratch_shapes=[pltpu.VMEM((512, 2048), BF)],
        compiler_params=params(16),
        cost_estimate=cost(805_000_000, 4 * MIB),
        name="moment",
    )(near, far, ctx_t)


def context_grad_kernel(*refs):
    near, far, wenc, out, flag, whole = refs
    flag[...] = jnp.zeros_like(flag)
    gather_rows(near, far, whole)
    out[...] = dot(whole[...], wenc[...], ((1,), (1,))).astype(BF)


def context_grad_of(near, far, wenc):
    return pl.pallas_call(
        context_grad_kernel,
        in_specs=vmem(3),
        out_specs=vmem(2),
        out_shape=[shape(512, 384), shape(8, 128, dtype=F32)],
        scratch_shapes=[pltpu.VMEM((512, 2048), BF)],
        compiler_params=params(16),
        cost_estimate=cost(805_000_000, 4 * MIB),
        name="context_grad",
    )(near, far, wenc)


def add_refs(*parts):
    return sum(p.astype(F32) for p in parts)


def second_x_kernel(a_keep, a_got, b_keep, b_got, after, a_send, b_send):
    a_send[...] = add_refs(a_keep[32:, :], a_got[32:, :]).astype(BF)
    b_send[...] = add_refs(b_keep[32:, :], b_got[32:, :]).astype(BF)


def second_x(a_keep, a_got, b_keep, b_got, after):
    return pl.pallas_call(
        second_x_kernel,
        in_specs=vmem(4) + any_space(1),
        out_specs=vmem(2),
        out_shape=[shape(32, 2048)] * 2,
        compiler_params=params(4),
        cost_estimate=cost(0, 1 * MIB),
        name="second_x",
    )(a_keep, a_got, b_keep, b_got, after)


def second_y_kernel(*refs):
    a_keep, a_got, a_last, b_keep, b_got, b_last = refs[:6]
    ma_keep, ma_got, mb_keep, mb_got = refs[6:10]
    far, near, a_send, b_send = refs[-4:]
    far[...] = add_refs(a_keep[:32, :], a_got[:32, :], a_last[...]).astype(BF)
    near[...] = add_refs(b_keep[:32, :], b_got[:32, :], b_last[...])
    a_send[...] = add_refs(ma_keep[384:, :], ma_got[384:, :]).astype(BF)
    b_send[...] = add_refs(mb_keep[384:, :], mb_got[384:, :]).astype(BF)


def second_y(*parts):
    return pl.pallas_call(
        second_y_kernel,
        in_specs=vmem(10) + any_space(len(parts) - 10),
        out_specs=vmem(4),
        out_shape=[shape(32, 2048), shape(32, 2048, dtype=F32)] + [shape(384, 256)] * 2,
        compiler_params=params(8),
        cost_estimate=cost(0, 2 * MIB),
        name="second_y",
    )(*parts)


def moment_sum_kernel(a_keep, a_got, a_last, b_keep, b_got, b_last, *outs):
    for n, refs in enumerate(((a_keep, a_got, a_last), (b_keep, b_got, b_last))):
        total = add_refs(refs[0][:384, :], refs[1][:384, :], refs[2][...]).astype(BF)
        outs[2 * n][...] = total[:, :128]
        outs[2 * n + 1][...] = total[:, 128:]


def moment_sum(*parts):
    return pl.pallas_call(
        moment_sum_kernel,
        in_specs=vmem(6),
        out_specs=vmem(4),
        out_shape=[shape(384, 128)] * 4,
        compiler_params=params(8),
        cost_estimate=cost(0, 2 * MIB),
        name="moment_sum",
    )(*parts)


def code_kernel(near, recv, after, code, *outs):
    code[...] = (near[...] + recv[...].astype(F32)).astype(BF)
    by_group(code, 128, outs)


def code_of(near, recv, after):
    return pl.pallas_call(
        code_kernel,
        in_specs=vmem(2) + any_space(1),
        out_specs=vmem(5),
        out_shape=[shape(32, 2048)] + [shape(32, 512)] * 4,
        compiler_params=params(8),
        cost_estimate=cost(0, 1 * MIB),
        name="code",
    )(near, recv, after)


def layer_out_kernel(code, dec, out):
    for g in range(GROUPS):
        out[:, g * 384:(g + 1) * 384] = dot(
            code[:, g * 128:(g + 1) * 128], dec[g * 128:(g + 1) * 128, :], ((1,), (0,))
        ).astype(BF)


def codec_grads_kernel(w_hbm, *refs):
    parts, codes, cots = refs[:4], refs[4:8], refs[8:12]
    total, own, other, enc_term, dec_term, w_block, sem = refs[12:]
    i, t = lax.axis_index("dp"), lax.axis_index("tensor")
    copy = pltpu.make_async_copy(w_hbm.at[:, ds(i, 384)], w_block, sem)
    copy.start()
    code = jnp.concatenate([r[...] for r in codes], axis=0)
    cot = jnp.concatenate([r[...] for r in cots], axis=0)
    dec_term[...] = dot(code, cot, ((0,), (0,)))
    total[...] = sum(r[...].astype(F32) for r in parts).astype(BF)
    copy.wait()
    enc_term[...] = dot(total[...], w_block[...], ((0,), (0,)))
    for dc, out in enumerate((own, other)):
        n = 0
        for dx in range(4):
            for dz in range(2):
                rows = ds(tadd(t, (dz, dx, dc)), 8)
                out[n:n + 8, :] = enc_term[rows, :]
                out[n + 8:n + 16, :] = dec_term[rows, :]
                n += 16


def w_out_grad_kernel(total, enc, out):
    i = lax.axis_index("dp")
    out[...] = dot(total[...], enc[ds(i, 128), :], ((1,), (0,)))


def add(*parts):
    return sum(p.astype(F32) for p in parts)


def on_device(ctx, w, enc, dec, cot):
    grad_code, *cots = pl.pallas_call(
        grad_code_kernel,
        in_specs=[pl.BlockSpec(memory_space=pltpu.HBM)] * 2,
        out_specs=vmem(5),
        out_shape=[shape(32, 2048)] + [shape(32, 1536)] * 4,
        scratch_shapes=[
            pltpu.VMEM((32, 6144), BF), pltpu.VMEM((2048, 384), BF),
            pltpu.SemaphoreType.DMA((5,)),
        ],
        compiler_params=pltpu.CompilerParams(vmem_limit_bytes=FIRST_VMEM),
        cost_estimate=cost(50_000_000, 2 * MIB),
        name="grad_code",
    )(cot, dec)

    theirs = fetch_tensor(grad_code, (1, 0, 0))
    cots = over_y(cots)
    wenc, ctx_t, ctx_r = wenc_of(w, ctx, enc, cots[1])

    own, other, pair, *cots = coded_of(ctx_r, wenc, grad_code, theirs, cots)
    pieces = [pair] + [fetch_tensor(pair, (0, k, 0)) for k in (1, 2, 3)]
    got = send_tensor(other, (0, 0, 1))
    cots = over_z(cots)

    packed, a_send, a_keep, b_send, b_keep = pack(pieces, own, got, *cots[1:])
    packed_far = send_tensor(packed, (0, 0, 1))
    a_got, b_got = swap_x(a_send, 1), swap_x(b_send, 3)

    ma_send, ma_keep, mb_send, mb_keep = moment(packed, packed_far, ctx_t)
    ma_got, mb_got = swap_y(ma_send, 1), swap_y(mb_send, 3)

    context_grad, flag = context_grad_of(packed, packed_far, wenc)
    a_send, b_send = second_x(a_keep, a_got, b_keep, b_got, ma_send)
    a_last, b_last = swap_x(a_send, 3), swap_x(b_send, 1)

    far, near, a_send, b_send = second_y(
        a_keep, a_got, a_last, b_keep, b_got, b_last, ma_keep, ma_got, mb_keep, mb_got, flag
    )
    recv = send_tensor(far, (1, 0, 0))
    ma_last, mb_last = swap_y(a_send, 3), swap_y(b_send, 1)

    subs = over_z(moment_sum(ma_keep, ma_got, ma_last, mb_keep, mb_got, mb_last))
    code, *codes = code_of(near, recv, subs[1])
    codes = over_z(code_regroup(over_y(codes)))

    layer_out = pl.pallas_call(
        layer_out_kernel,
        in_specs=vmem(2),
        out_specs=vmem(1)[0],
        out_shape=shape(32, 6144),
        compiler_params=params(8),
        cost_estimate=cost(50_000_000, 2 * MIB),
        name="layer_out",
    )(code, dec)

    total, own, other = pl.pallas_call(
        codec_grads_kernel,
        in_specs=[pl.BlockSpec(memory_space=pltpu.HBM)] + vmem(12),
        out_specs=vmem(3),
        out_shape=[shape(384, 128)] + [shape(128, 384, dtype=F32)] * 2,
        scratch_shapes=[
            pltpu.VMEM((128, 384), F32), pltpu.VMEM((128, 384), F32),
            pltpu.VMEM((384, 384), BF), pltpu.SemaphoreType.DMA,
        ],
        compiler_params=params(8),
        cost_estimate=cost(100_000_000, 2 * MIB),
        name="codec_grads",
    )(w, *subs, *codes, *cots)
    got = send_tensor(other, (0, 0, 1))
    part = [add(own[32 * k:32 * k + 32], got[32 * k:32 * k + 32]) for k in range(4)]
    rows = [part[0]] + [send_tensor(part[k], (0, k, 0)) for k in (2, 1, 3)]
    far = add(*[r[16:] for r in rows])
    near = add(*[r[:16] for r in rows])
    grads = near + send_tensor(far, (1, 0, 0))
    encoder_grad, decoder_grad = grads[:8], grads[8:]
    w_out_grad = pl.pallas_call(
        w_out_grad_kernel,
        in_specs=vmem(2),
        out_specs=vmem(1)[0],
        out_shape=shape(384, 384, dtype=F32),
        compiler_params=params(8),
        cost_estimate=cost(50_000_000, 2 * MIB),
        name="w_out_grad",
    )(total, enc)
    return layer_out, context_grad, w_out_grad, encoder_grad, decoder_grad


def solution(mesh):
    placed = (P("dp", "tensor"), P("tensor", None), P(), P(), P(("dp", "tensor"), None))
    return jax.shard_map(
        on_device,
        mesh=mesh,
        in_specs=placed,
        out_specs=(
            P(("dp", "tensor"), None),
            P("dp", "tensor"),
            P("tensor", "dp"),
            P(("dp", "tensor"), None),
            P(("dp", "tensor"), None),
        ),
        check_vma=False,
    )
```
